256 devices in a mesh: req: 8 (over y, core), kv: 32 (over z, x).
Axes of the slice: x: 4, y: 4, z: 8, core: 2. Of those that a mesh axis runs over, the one named last changes fastest.
Arguments:
- q_nope: bfloat16 [32, 128, 128], P('req', 'kv'), may hold values from -6 to 6
- q_rope: bfloat16 [32, 128, 64], P('req', 'kv'), may hold values from -8 to 8
- cache: bfloat16 [32, 65536, 576], P('req', 'kv'), may hold values from -14 to 14
- lengths: int32 [32], P('req'), may hold values from 2 to 65536, as said below
- w_uk: bfloat16 [128, 128, 512], P('kv'), may hold values from -0.5 to 0.5
- w_uv: bfloat16 [128, 512, 128], P('kv'), may hold values from -0.25 to 0.25
Outputs:
- attn: bfloat16 [32, 16384], P('req', 'kv')
The draws below stay inside these ranges and needn't reach their ends.
Inputs may be any that keep to these rules, and one draw needn't show every extreme that they name: `lengths`: some request has exactly 65536.
All inputs are finite; a program needn't handle non-finite values.
Results may differ from the reference program's by a relative error of at most 0.0084.
Values may be sent and summed in bfloat16 or wider, within the bound.
A program may use at most 128 MiB of HBM per device.

```python
import math
import jax
import jax.numpy as jnp
from jax import lax

H = 128
C = 512
R = 64
DN = 128
DV = 128
SPLIT = 2048
B = 32
S = 65536


def draw_q_rope(key, part):
    key = jax.random.fold_in(key, 3)
    values = jnp.clip(jax.random.normal(key, (B, H, R), jnp.float32), -6.0, 6.0)
    return values.astype(jnp.bfloat16)


def draw_cache(key, part):
    key = jax.random.fold_in(key, 5)
    row_scales = jnp.exp(jax.random.uniform(jax.random.fold_in(key, 1), (B, S, 1), jnp.float32, math.log(0.35), math.log(3.5)))
    latent = jnp.clip(jax.random.normal(key, (B, S, C), jnp.float32), -4.0, 4.0) * row_scales
    rope = jnp.clip(jax.random.normal(jax.random.fold_in(key, 3), (B, S, R), jnp.float32), -4.0, 4.0)
    return jnp.concatenate([latent, rope], axis=2).astype(jnp.bfloat16)


def draw_lengths(key, part):
    key = jax.random.fold_in(key, 7)
    values = jax.random.randint(key, (B,), 2, S + 1)
    picked = jax.random.randint(jax.random.fold_in(key, 1), (), 0, B)
    return values.at[picked].set(S).astype(jnp.int32)


def shard_levels(own_key, extent, pieces, low, high):
    factor_of, own = 1.0, jax.random.fold_in(own_key, 6)
    for position, shards_of in pieces:
        steps = jnp.exp(jax.random.uniform(jax.random.fold_in(own, position), (shards_of,), jnp.float32, low / len(pieces), high / len(pieces)))
        factor_of = factor_of * jnp.repeat(steps, extent[position] // shards_of).reshape([-1 if axis == position else 1 for axis in range(len(extent))])
    return factor_of


def gaussian(key, extent, scale, limit, pieces=(), kind=jnp.bfloat16):
    array = scale * jax.random.normal(key, extent, jnp.float32)
    if pieces:
        array = array * shard_levels(key, extent, pieces, -0.22, 0.18)
    return jnp.clip(array, -limit, limit).astype(kind)


def setup_inputs(seed: int = 0) -> dict:
    arg_keys = jax.random.split(jax.random.key(seed), 7)
    return {
        "q_nope": gaussian(arg_keys[0], (B, H, DN), 1.0, 6.0, ((0, 8), (1, 32))),
        "q_rope": draw_q_rope(jax.random.fold_in(arg_keys[6], 71), 0),
        "cache": draw_cache(jax.random.fold_in(arg_keys[6], 71), 0),
        "lengths": draw_lengths(jax.random.fold_in(arg_keys[6], 71), 0),
        "w_uk": gaussian(arg_keys[4], (H, DN, C), DN ** -0.5, 0.5, ((0, 32),)),
        "w_uv": gaussian(arg_keys[5], (H, C, DV), C ** -0.5, 0.25, ((0, 32),)),
    }


def reference(q_nope, q_rope, cache, lengths, w_uk, w_uv):
    score_scale = (DN + R) ** -0.5
    q_lat = jnp.einsum('bhd,hdc->bhc', q_nope.astype(jnp.float32), w_uk.astype(jnp.float32)).astype(jnp.bfloat16)
    q_full = jnp.concatenate([q_lat, q_rope], axis=2)
    splits = S // SPLIT
    blocks = cache.reshape(B, splits, SPLIT, C + R)

    def one_request(items):
        query_rows, cache_blocks, length_one = items

        def one_split(pair):
            block, index = pair
            scores = jnp.dot(query_rows, block.T, preferred_element_type=jnp.float32) * score_scale
            positions = index * SPLIT + jnp.arange(SPLIT, dtype=jnp.int32)
            is_live = positions[None, :] < length_one
            scores = jnp.where(is_live, scores, jnp.float32(-1e30))
            split_max = jnp.max(scores, axis=1)
            expo = jnp.where(is_live, jnp.exp(scores - split_max[:, None]), jnp.float32(0.0))
            split_sum = jnp.sum(expo, axis=1)
            split_out = jnp.dot(expo.astype(jnp.bfloat16), block[:, :C], preferred_element_type=jnp.float32)
            return split_max, split_sum, split_out

        maxima, sums, outs = lax.map(one_split, (cache_blocks, jnp.arange(splits, dtype=jnp.int32)))
        top_score = jnp.max(maxima, axis=0)
        factor = jnp.exp(maxima - top_score[None, :])
        denominator = jnp.sum(factor * sums, axis=0)
        numerator = jnp.sum(factor[:, :, None] * outs, axis=0)
        return (numerator / denominator[:, None]).astype(jnp.bfloat16)

    latent_out = lax.map(one_request, (q_full, blocks, lengths))
    attn = jnp.einsum('bhc,hcv->bhv', latent_out.astype(jnp.float32), w_uv.astype(jnp.float32))
    return attn.astype(jnp.bfloat16).reshape(B, H * DV)
```

```python
import functools
import math

import jax
import jax.numpy as jnp
from jax import lax
from jax.experimental import pallas as pl
from jax.experimental.pallas import tpu as pltpu
from jax.sharding import PartitionSpec as P

MESH = pl.DeviceIdType.MESH
F32 = jnp.float32
BF16 = jnp.bfloat16
NX, NZ = 4, 8
NB, NH = 4, 4
LANES = 128
DEAD = -1e30
CHUNK = 512


def stats_tile(top, total):
    lane = lax.broadcasted_iota(jnp.int32, (top.shape[0], LANES), 1)
    top_hi = top.astype(BF16).astype(F32)
    sum_hi = total.astype(BF16).astype(F32)
    first = jnp.where(lane < 32, top_hi, top - top_hi)
    second = jnp.where(lane < 96, sum_hi, total - sum_hi)
    return jnp.where(lane < 64, first, second)


def read_stats(tile):
    return tile[:, 0:1] + tile[:, 32:33], tile[:, 64:65] + tile[:, 96:97]


def kernel(
    scale,
    lengths,
    q_nope,
    q_rope,
    w_uk_hbm,
    w_uv_hbm,
    cache_hbm,
    out,
    w_uk,
    w_uv,
    cache,
    gathered,
    flat,
    rope_flat,
    query,
    scores,
    probs,
    x_send,
    x_recv,
    turn,
    z_send,
    z_recv,
    latent,
    local_sem,
    gz_send_sem,
    gz_recv_sem,
    gx_send_sem,
    gx_recv_sem,
    rx_send_sem,
    rx_recv_sem,
    rz_send_sem,
    rz_recv_sem,
):
    req = lax.axis_index("req")
    kv = lax.axis_index("kv")
    z = lax.div(kv, NX)
    x = lax.rem(kv, NX)
    split_len = cache.shape[2]
    latent_width = w_uk.shape[2]
    z_order = (4, 3, 5, 2, 6, 1, 7)
    x_order = (2, 1, 3)

    def z_at(d):
        return lax.rem(z + d, NZ)

    def x_at(d):
        return lax.rem(x + d, NX)

    barrier = pltpu.get_barrier_semaphore()
    for d in z_order:
        pl.semaphore_signal(barrier, inc=1, device_id=(req, z_at(d) * NX + x), device_id_type=MESH)
    for d in x_order:
        pl.semaphore_signal(barrier, inc=1, device_id=(req, z * NX + x_at(d)), device_id_type=MESH)

    uk_copy = pltpu.make_async_copy(w_uk_hbm, w_uk, local_sem.at[4])
    uk_copy.start()

    def cache_copy(b):
        return pltpu.make_async_copy(cache_hbm.at[b], cache.at[b], local_sem.at[b])

    for b in range(NB):
        cache_copy(b).start()
    uv_copy = pltpu.make_async_copy(w_uv_hbm, w_uv, local_sem.at[5])
    uv_copy.start()

    def gz_copy(b, source, d):
        return pltpu.make_async_remote_copy(
            src_ref=gathered.at[b, x, source],
            dst_ref=gathered.at[b, x, source],
            send_sem=gz_send_sem.at[b, d],
            recv_sem=gz_recv_sem.at[b, source],
            device_id=(req, z_at(d) * NX + x),
            device_id_type=MESH,
        )

    def gx_copy(b, source, d):
        return pltpu.make_async_remote_copy(
            src_ref=gathered.at[b, source],
            dst_ref=gathered.at[b, source],
            send_sem=gx_send_sem.at[b, d],
            recv_sem=gx_recv_sem.at[b, source],
            device_id=(req, z * NX + x_at(d)),
            device_id_type=MESH,
        )

    def rx_copy(b, source, d):
        return pltpu.make_async_remote_copy(
            src_ref=x_send.at[b, pl.ds(pl.multiple_of(x_at(d) * 32, 32), 32)],
            dst_ref=x_recv.at[b, source],
            send_sem=rx_send_sem.at[b, d],
            recv_sem=rx_recv_sem.at[b, source],
            device_id=(req, z * NX + x_at(d)),
            device_id_type=MESH,
        )

    def rz_copy(b, source, d):
        return pltpu.make_async_remote_copy(
            src_ref=z_send.at[b, z_at(d)],
            dst_ref=z_recv.at[b, source],
            send_sem=rz_send_sem.at[b, d],
            recv_sem=rz_recv_sem.at[b, source],
            device_id=(req, z_at(d) * NX + x),
            device_id_type=MESH,
        )

    rope_flat[0:16, :] = jnp.zeros((16, LANES), F32)
    for b in range(NB):
        flat[b * NH : (b + 1) * NH, :] = q_nope[b].astype(F32)
        rope_flat[b * NH : (b + 1) * NH, 0:64] = q_rope[b].astype(F32)
    gathered[NB, x, z] = rope_flat[0:16, :].astype(BF16)
    rows = flat[0:16, :]
    head = lax.rem(lax.broadcasted_iota(jnp.int32, (16, LANES), 0), NH)
    uk_copy.wait()
    q_lat = jnp.zeros((16, latent_width), F32)
    for h in range(NH):
        own = jnp.where(head == h, rows, 0.0).astype(BF16)
        q_lat = q_lat + jnp.dot(own, w_uk[h], preferred_element_type=F32)
    for b in range(NB):
        for j in range(4):
            flat[b * 16 + j * NH : b * 16 + (j + 1) * NH, :] = q_lat[
                b * NH : (b + 1) * NH, j * LANES : (j + 1) * LANES
            ]
    for b in range(NB):
        gathered[b, x, z] = flat[b * 16 : (b + 1) * 16, :].astype(BF16)

    pl.semaphore_wait(barrier, NZ - 1 + NX - 1)

    for b in (NB, 0, 1, 2, 3):
        for d in z_order:
            gz_copy(b, z, d).start()
    for b in (NB, 0, 1, 2, 3):
        for d in z_order:
            gz_copy(b, z_at(d), d).wait_recv()
        for d in x_order:
            gx_copy(b, x, d).start()

    for d in x_order:
        gx_copy(NB, x_at(d), d).wait_recv()
    rope_flat[...] = gathered[NB].reshape(NX * NZ * 16, LANES).astype(F32)

    position = kv * split_len + lax.broadcasted_iota(jnp.int32, (1, CHUNK), 1)

    def attend(b, carry):
        for d in x_order:
            gx_copy(b, x_at(d), d).wait_recv()
        flat[...] = gathered[b].reshape(NX * NZ * 16, LANES).astype(F32)
        for xs in range(NX):
            for hp in range(0, NH, 2):
                at = xs * 32 + hp * 8
                for j in range(4):
                    pair = [
                        flat[pl.ds(xs * 128 + j * NH + h, 8, stride=16), :] for h in (hp, hp + 1)
                    ]
                    query[at : at + 16, j * LANES : (j + 1) * LANES] = jnp.concatenate(
                        pair, axis=0
                    ).astype(BF16)
                pair = [
                    rope_flat[pl.ds(xs * 128 + b * NH + h, 8, stride=16), :] for h in (hp, hp + 1)
                ]
                query[at : at + 16, 512:640] = jnp.concatenate(pair, axis=0).astype(BF16)
        cache_copy(b).wait()
        q = query[:, 0:576]
        length = lengths[b]
        peak = None
        for c in range(0, split_len, CHUNK):
            s = jnp.dot(q, cache[b, :, c : c + CHUNK], preferred_element_type=F32)
            s = jnp.where(position + c < length, s, DEAD)
            scores[:, c : c + CHUNK] = s
            for k in range(0, CHUNK, LANES):
                piece = s[:, k : k + LANES]
                peak = piece if peak is None else jnp.maximum(peak, piece)
        top = jnp.max(peak, axis=1, keepdims=True) * scale
        top_hi = top.astype(BF16).astype(F32)
        top = top_hi + (top - top_hi).astype(BF16).astype(F32)
        total = jnp.zeros((128, LANES), F32)
        for c in range(0, split_len, CHUNK):
            p = jnp.exp2(scores[:, c : c + CHUNK] * scale - top)
            probs[:, c : c + CHUNK] = p.astype(BF16)
            for k in range(0, CHUNK, LANES):
                total = total + p[:, k : k + LANES]
        o = lax.dot_general(
            probs[...], cache[b, 0:512, :], (((1,), (1,)), ((), ())), preferred_element_type=F32
        )
        x_send[b, :, 0:512] = o.astype(BF16)
        x_send[b, :, 512:640] = stats_tile(top, jnp.sum(total, axis=1, keepdims=True)).astype(BF16)
        for d in x_order:
            rx_copy(b, x, d).start()
        return carry

    lax.fori_loop(0, NB, attend, 0)

    def reduce_x(b, carry):
        for d in x_order:
            rx_copy(b, x_at(d), d).wait_recv()
        parts = [x_send[b, pl.ds(pl.multiple_of(x * 32, 32), 32), :].astype(F32)]
        for d in x_order:
            parts.append(x_recv[b, x_at(d)].astype(F32))
        stats = [read_stats(part[:, 512:640]) for part in parts]
        top = functools.reduce(jnp.maximum, [t for t, _ in stats])
        acc, total = None, None
        for part, (t, s) in zip(parts, stats):
            w = jnp.exp2(t - top)
            acc = part[:, 0:512] * w if acc is None else acc + part[:, 0:512] * w
            total = s * w if total is None else total + s * w
        info = stats_tile(top, total)
        for h in range(NH):
            for j in range(4):
                r = h * 4 + j
                turn[r * 8 : r * 8 + 8, :] = acc[h * 8 : h * 8 + 8, j * LANES : (j + 1) * LANES]
                turn[128 + r * 8 : 128 + r * 8 + 8, :] = info[h * 8 : h * 8 + 8, :]
        for zs in range(NZ):
            z_send[b, zs] = turn[pl.ds(zs, 32, stride=8), :].astype(BF16)
        for d in z_order:
            rz_copy(b, z, d).start()
        return carry

    lax.fori_loop(0, NB, reduce_x, 0)

    def reduce_z(b, carry):
        for d in z_order:
            rz_copy(b, z_at(d), d).wait_recv()
        parts = [z_send[b, z].astype(F32)] + [z_recv[b, z_at(d)].astype(F32) for d in z_order]
        stats = [read_stats(part[16:32]) for part in parts]
        top = functools.reduce(jnp.maximum, [t for t, _ in stats])
        acc, total = None, None
        for part, (t, s) in zip(parts, stats):
            w = jnp.exp2(t - top)
            acc = part[0:16] * w if acc is None else acc + part[0:16] * w
            total = s * w if total is None else total + s * w
        latent[pl.ds(pl.multiple_of(b * 16, 16), 16), :] = acc / total
        return carry

    lax.fori_loop(0, NB, reduce_z, 0)

    uv_copy.wait()
    for h in range(NH):
        lat = jnp.concatenate(
            [latent[pl.ds(h * 4 + j, NB, stride=16), :] for j in range(4)], axis=1
        ).astype(BF16)
        out[:, h * LANES : (h + 1) * LANES] = jnp.dot(
            lat, w_uv[h], preferred_element_type=F32
        ).astype(BF16)

    def drain(b, carry):
        for d in z_order:
            gz_copy(b, z, d).wait_send()
            rz_copy(b, z, d).wait_send()
        for d in x_order:
            gx_copy(b, x, d).wait_send()
            rx_copy(b, x, d).wait_send()
        return carry

    lax.fori_loop(0, NB, drain, 0)
    for d in z_order:
        gz_copy(NB, z, d).wait_send()
    for d in x_order:
        gx_copy(NB, x, d).wait_send()


def local(q_nope, q_rope, cache, lengths, w_uk, w_uv):
    scale = (q_nope.shape[2] + q_rope.shape[2]) ** (-0.5) * math.log2(math.e)
    cache_t = jnp.swapaxes(cache, 1, 2)
    vmem = pl.BlockSpec(memory_space=pltpu.VMEM)
    hbm = pl.BlockSpec(memory_space=pl.ANY)
    dma = pltpu.SemaphoreType.DMA
    return pl.pallas_call(
        functools.partial(kernel, scale),
        out_shape=jax.ShapeDtypeStruct((NB, NH * w_uv.shape[2]), BF16),
        in_specs=[pl.BlockSpec(memory_space=pltpu.SMEM), vmem, vmem, hbm, hbm, hbm],
        out_specs=vmem,
        scratch_shapes=[
            pltpu.VMEM(w_uk.shape, BF16),
            pltpu.VMEM(w_uv.shape, BF16),
            pltpu.VMEM(cache_t.shape, BF16),
            pltpu.VMEM((NB + 1, NX, NZ, 16, LANES), BF16),
            pltpu.VMEM((NX * NZ * 16, LANES), F32),
            pltpu.VMEM((NX * NZ * 16, LANES), F32),
            pltpu.VMEM((128, 640), BF16),
            pltpu.VMEM((128, cache_t.shape[2]), F32),
            pltpu.VMEM((128, cache_t.shape[2]), BF16),
            pltpu.VMEM((NB, 128, 640), BF16),
            pltpu.VMEM((NB, NX, 32, 640), BF16),
            pltpu.VMEM((256, LANES), F32),
            pltpu.VMEM((NB, NZ, 32, LANES), BF16),
            pltpu.VMEM((NB, NZ, 32, LANES), BF16),
            pltpu.VMEM((NB * 16, LANES), F32),
            dma((6,)),
            dma((NB + 1, NZ)),
            dma((NB + 1, NZ)),
            dma((NB + 1, NX)),
            dma((NB + 1, NX)),
            dma((NB, NX)),
            dma((NB, NX)),
            dma((NB, NZ)),
            dma((NB, NZ)),
        ],
        compiler_params=pltpu.CompilerParams(
            collective_id=0, has_side_effects=True, vmem_limit_bytes=48 * 2**20
        ),
    )(lengths, q_nope, q_rope, w_uk, w_uv, cache_t)


def solution(mesh):
    in_specs = (
        P("req", "kv", None),
        P("req", "kv", None),
        P("req", "kv", None),
        P("req"),
        P("kv", None, None),
        P("kv", None, None),
    )
    return jax.shard_map(
        local, mesh=mesh, in_specs=in_specs, out_specs=P("req", "kv"), check_vma=False
    )
```

```python
import functools
import math

import jax
import jax.numpy as jnp
from jax import lax
from jax.experimental import pallas as pl
from jax.experimental.pallas import tpu as pltpu
from jax.sharding import PartitionSpec as P

MESH = pl.DeviceIdType.MESH
F32 = jnp.float32
BF16 = jnp.bfloat16
NX, NZ = 4, 8
NB, NH = 4, 4
LANES = 128
DEAD = -1e30
CHUNK = 512


def to_lanes(column, rows):
    row = lax.broadcasted_iota(jnp.int32, (rows, LANES), 0)
    lane = lax.broadcasted_iota(jnp.int32, (rows, LANES), 1)
    return jnp.sum(jnp.where(row == lane, column, 0.0), axis=0, keepdims=True)


def to_column(row, picked):
    return jnp.sum(jnp.where(picked, row, 0.0), axis=1, keepdims=True)


def kernel(
    scale,
    lengths_hbm,
    q_nope_hbm,
    q_rope_hbm,
    w_uk_hbm,
    w_uv_hbm,
    cache_hbm,
    out,
    lengths,
    q_nope,
    q_rope,
    w_uk,
    w_uv,
    cache,
    gathered,
    ropes,
    flat,
    rope_flat,
    query,
    scores,
    probs,
    x_send,
    x_recv,
    x_stat,
    turn,
    z_send,
    z_recv,
    z_stat,
    latent,
    local_sem,
    send_sem,
    gz_sem,
    gx_sem,
    rx_sem,
    rz_sem,
    rxs_sem,
    rzs_sem,
):
    req = lax.axis_index("req")
    kv = lax.axis_index("kv")
    z = lax.div(kv, NX)
    x = lax.rem(kv, NX)
    split_len = cache.shape[2]
    latent_width = w_uk.shape[2]
    z_order = (4, 3, 5, 2, 6, 1, 7)
    x_order = (2, 1, 3)

    def z_at(d):
        return lax.rem(z + d, NZ)

    def x_at(d):
        return lax.rem(x + d, NX)

    barrier = pltpu.get_barrier_semaphore()
    for d in z_order:
        pl.semaphore_signal(barrier, inc=1, device_id=(req, z_at(d) * NX + x), device_id_type=MESH)
    for d in x_order:
        pl.semaphore_signal(barrier, inc=1, device_id=(req, z * NX + x_at(d)), device_id_type=MESH)

    first_copies = [
        pltpu.make_async_copy(q_rope_hbm, q_rope, local_sem.at[6]),
        pltpu.make_async_copy(q_nope_hbm, q_nope, local_sem.at[7]),
        pltpu.make_async_copy(w_uk_hbm, w_uk, local_sem.at[4]),
    ]
    for copy in first_copies:
        copy.start()
    lengths_copy = pltpu.make_async_copy(lengths_hbm, lengths, local_sem.at[8])
    lengths_copy.start()

    def cache_copy(b):
        return pltpu.make_async_copy(cache_hbm.at[b], cache.at[b], local_sem.at[b])

    for b in range(NB):
        cache_copy(b).start()
    uv_copy = pltpu.make_async_copy(w_uv_hbm, w_uv, local_sem.at[5])
    uv_copy.start()

    def to_z(src, dst, kind, sem, d):
        return pltpu.make_async_remote_copy(
            src_ref=src,
            dst_ref=dst,
            send_sem=send_sem.at[kind],
            recv_sem=sem,
            device_id=(req, z_at(d) * NX + x),
            device_id_type=MESH,
        )

    def to_x(src, dst, kind, sem, d):
        return pltpu.make_async_remote_copy(
            src_ref=src,
            dst_ref=dst,
            send_sem=send_sem.at[kind],
            recv_sem=sem,
            device_id=(req, z * NX + x_at(d)),
            device_id_type=MESH,
        )

    def take(ref, sem):
        pltpu.make_async_copy(ref, ref, sem).wait()

    for copy in first_copies:
        copy.wait()
    for b in range(NB):
        flat[b * NH : (b + 1) * NH, :] = q_nope[b].astype(F32)
        rope = q_rope[b].astype(F32)
        for h in range(NH):
            r = b * 2 + h // 2
            rope_flat[r : r + 1, (h % 2) * 64 : (h % 2) * 64 + 64] = rope[h : h + 1, :]
    ropes[x, z] = rope_flat[0:8, :].astype(BF16)
    rows = flat[0:16, :]
    head = lax.rem(lax.broadcasted_iota(jnp.int32, (16, LANES), 0), NH)
    q_lat = jnp.zeros((16, latent_width), F32)
    for h in range(NH):
        own = jnp.where(head == h, rows, 0.0).astype(BF16)
        q_lat = q_lat + jnp.dot(own, w_uk[h], preferred_element_type=F32)
    for b in range(NB):
        for j in range(4):
            flat[b * 16 + j * NH : b * 16 + (j + 1) * NH, :] = q_lat[
                b * NH : (b + 1) * NH, j * LANES : (j + 1) * LANES
            ]
    for b in range(NB):
        gathered[b, x, z] = flat[b * 16 : (b + 1) * 16, :].astype(BF16)

    pl.semaphore_wait(barrier, NZ - 1 + NX - 1)

    for d in z_order:
        to_z(ropes.at[x, z], ropes.at[x, z], 1, gz_sem.at[NB], d).start()
    for b in range(NB):
        for d in z_order:
            to_z(gathered.at[b, x, z], gathered.at[b, x, z], 0, gz_sem.at[b], d).start()
    take(ropes.at[0, pl.ds(0, NZ - 1)], gz_sem.at[NB])
    for d in x_order:
        to_x(ropes.at[x], ropes.at[x], 3, gx_sem.at[NB], d).start()
    for b in range(NB):
        take(gathered.at[b, 0, pl.ds(0, NZ - 1)], gz_sem.at[b])
        for d in x_order:
            to_x(gathered.at[b, x], gathered.at[b, x], 2, gx_sem.at[b], d).start()

    take(ropes.at[pl.ds(0, NX - 1)], gx_sem.at[NB])
    rope_flat[...] = ropes[...].reshape(NX * NZ * 8, LANES).astype(F32)

    lengths_copy.wait()
    position = kv * split_len + lax.broadcasted_iota(jnp.int32, (1, CHUNK), 1)

    def attend(b, carry):
        take(gathered.at[b, pl.ds(0, NX - 1)], gx_sem.at[b])
        flat[...] = gathered[b].reshape(NX * NZ * 16, LANES).astype(F32)
        for xs in range(NX):
            for hp in range(0, NH, 2):
                at = xs * 32 + hp * 8
                for j in range(4):
                    pair = [
                        flat[pl.ds(xs * 128 + j * NH + h, 8, stride=16), :] for h in (hp, hp + 1)
                    ]
                    query[at : at + 16, j * LANES : (j + 1) * LANES] = jnp.concatenate(
                        pair, axis=0
                    ).astype(BF16)
                both = rope_flat[pl.ds(xs * 64 + b * 2 + hp // 2, 8, stride=8), :]
                query[at : at + 16, 512:576] = jnp.concatenate(
                    [both[:, 0:64], both[:, 64:128]], axis=0
                ).astype(BF16)
        cache_copy(b).wait()
        q = query[...]
        length = lengths[b]
        peak = None
        for c in range(0, split_len, CHUNK):
            s = jnp.dot(q, cache[b, :, c : c + CHUNK], preferred_element_type=F32)
            s = jnp.where(position + c < length, s, DEAD)
            scores[:, c : c + CHUNK] = s
            for k in range(0, CHUNK, LANES):
                piece = s[:, k : k + LANES]
                peak = piece if peak is None else jnp.maximum(peak, piece)
        top = jnp.max(peak, axis=1, keepdims=True) * scale
        total = jnp.zeros((128, LANES), F32)
        for c in range(0, split_len, CHUNK):
            p = jnp.exp2(scores[:, c : c + CHUNK] * scale - top)
            probs[:, c : c + CHUNK] = p.astype(BF16)
            for k in range(0, CHUNK, LANES):
                total = total + p[:, k : k + LANES]
        o = lax.dot_general(
            probs[...], cache[b, 0:512, :], (((1,), (1,)), ((), ())), preferred_element_type=F32
        )
        x_send[b] = o.astype(BF16)
        x_stat[b, x, 0:1, :] = to_lanes(top, 128)
        x_stat[b, x, 1:2, :] = to_lanes(jnp.sum(total, axis=1, keepdims=True), 128)
        for d in x_order:
            to_x(x_stat.at[b, x], x_stat.at[b, x], 5, rxs_sem.at[b], d).start()
            rows_there = pl.ds(pl.multiple_of(x_at(d) * 32, 32), 32)
            to_x(x_send.at[b, rows_there], x_recv.at[b, x], 4, rx_sem.at[b], d).start()
        return carry

    lax.fori_loop(0, NB, attend, 0)

    def reduce_x(b, carry):
        take(x_stat.at[b, pl.ds(0, NX - 1)], rxs_sem.at[b])
        take(x_recv.at[b, pl.ds(0, NX - 1)], rx_sem.at[b])
        row = lax.broadcasted_iota(jnp.int32, (32, LANES), 0)
        lane = lax.broadcasted_iota(jnp.int32, (32, LANES), 1)
        picked = lane == row + x * 32
        tops, sums = [], []
        for d in (0,) + x_order:
            stat = x_stat[b, x_at(d)]
            tops.append(to_column(stat[0:1, :], picked))
            sums.append(to_column(stat[1:2, :], picked))
        top = functools.reduce(jnp.maximum, tops)
        weights = [jnp.exp2(t - top) for t in tops]
        total = sum(w * s for w, s in zip(weights, sums))
        z_stat[b, z, 0:1, :] = to_lanes(top, 32)
        z_stat[b, z, 1:2, :] = to_lanes(total, 32)
        acc = x_send[b, pl.ds(pl.multiple_of(x * 32, 32), 32), :].astype(F32) * weights[0]
        for d, w in zip(x_order, weights[1:]):
            acc = acc + x_recv[b, x_at(d)].astype(F32) * w
        for h in range(NH):
            for j in range(4):
                r = h * 4 + j
                turn[r * 8 : r * 8 + 8, :] = acc[h * 8 : h * 8 + 8, j * LANES : (j + 1) * LANES]
        for zs in range(NZ):
            z_send[b, zs] = turn[pl.ds(zs, 16, stride=8), :].astype(BF16)
        for d in z_order:
            to_z(z_stat.at[b, z], z_stat.at[b, z], 7, rzs_sem.at[b], d).start()
            to_z(z_send.at[b, z_at(d)], z_recv.at[b, z], 6, rz_sem.at[b], d).start()
        return carry

    lax.fori_loop(0, NB, reduce_x, 0)

    def reduce_z(b, carry):
        take(z_stat.at[b, pl.ds(0, NZ - 1)], rzs_sem.at[b])
        take(z_recv.at[b, pl.ds(0, NZ - 1)], rz_sem.at[b])
        row = lax.broadcasted_iota(jnp.int32, (16, LANES), 0)
        lane = lax.broadcasted_iota(jnp.int32, (16, LANES), 1)
        picked = lane == lax.div(row, 4) * 8 + z
        tops, sums = [], []
        for d in (0,) + z_order:
            stat = z_stat[b, z_at(d)]
            tops.append(to_column(stat[0:1, :], picked))
            sums.append(to_column(stat[1:2, :], picked))
        top = functools.reduce(jnp.maximum, tops)
        weights = [jnp.exp2(t - top) for t in tops]
        total = sum(w * s for w, s in zip(weights, sums))
        acc = z_send[b, z].astype(F32) * weights[0]
        for d, w in zip(z_order, weights[1:]):
            acc = acc + z_recv[b, z_at(d)].astype(F32) * w
        latent[pl.ds(pl.multiple_of(b * 16, 16), 16), :] = acc / total
        return carry

    lax.fori_loop(0, NB, reduce_z, 0)

    uv_copy.wait()
    for h in range(NH):
        lat = jnp.concatenate(
            [latent[pl.ds(h * 4 + j, NB, stride=16), :] for j in range(4)], axis=1
        ).astype(BF16)
        out[:, h * LANES : (h + 1) * LANES] = jnp.dot(
            lat, w_uv[h], preferred_element_type=F32
        ).astype(BF16)

    take(gathered.at[pl.ds(0, NB), 0, pl.ds(0, NZ - 1)], send_sem.at[0])
    take(ropes.at[0, pl.ds(0, NZ - 1)], send_sem.at[1])
    take(gathered.at[pl.ds(0, NB), pl.ds(0, NX - 1)], send_sem.at[2])
    take(ropes.at[pl.ds(0, NX - 1)], send_sem.at[3])
    take(x_recv.at[pl.ds(0, NB), pl.ds(0, NX - 1)], send_sem.at[4])
    take(x_stat.at[pl.ds(0, NB), pl.ds(0, NX - 1)], send_sem.at[5])
    take(z_recv.at[pl.ds(0, NB), pl.ds(0, NZ - 1)], send_sem.at[6])
    take(z_stat.at[pl.ds(0, NB), pl.ds(0, NZ - 1)], send_sem.at[7])


def local(q_nope, q_rope, cache, lengths, w_uk, w_uv):
    scale = (q_nope.shape[2] + q_rope.shape[2]) ** (-0.5) * math.log2(math.e)
    cache_t = jnp.swapaxes(cache, 1, 2)
    vmem = pl.BlockSpec(memory_space=pltpu.VMEM)
    hbm = pl.BlockSpec(memory_space=pl.ANY)
    dma = pltpu.SemaphoreType.DMA
    return pl.pallas_call(
        functools.partial(kernel, scale),
        out_shape=jax.ShapeDtypeStruct((NB, NH * w_uv.shape[2]), BF16),
        in_specs=[hbm] * 6,
        out_specs=vmem,
        scratch_shapes=[
            pltpu.SMEM(lengths.shape, jnp.int32),
            pltpu.VMEM(q_nope.shape, BF16),
            pltpu.VMEM(q_rope.shape, BF16),
            pltpu.VMEM(w_uk.shape, BF16),
            pltpu.VMEM(w_uv.shape, BF16),
            pltpu.VMEM(cache_t.shape, BF16),
            pltpu.VMEM((NB, NX, NZ, 16, LANES), BF16),
            pltpu.VMEM((NX, NZ, 8, LANES), BF16),
            pltpu.VMEM((NX * NZ * 16, LANES), F32),
            pltpu.VMEM((NX * NZ * 8, LANES), F32),
            pltpu.VMEM((128, 576), BF16),
            pltpu.VMEM((128, cache_t.shape[2]), F32),
            pltpu.VMEM((128, cache_t.shape[2]), BF16),
            pltpu.VMEM((NB, 128, 512), BF16),
            pltpu.VMEM((NB, NX, 32, 512), BF16),
            pltpu.VMEM((NB, NX, 2, LANES), F32),
            pltpu.VMEM((128, LANES), F32),
            pltpu.VMEM((NB, NZ, 16, LANES), BF16),
            pltpu.VMEM((NB, NZ, 16, LANES), BF16),
            pltpu.VMEM((NB, NZ, 2, LANES), F32),
            pltpu.VMEM((NB * 16, LANES), F32),
            dma((9,)),
            dma((8,)),
            dma((NB + 1,)),
            dma((NB + 1,)),
            dma((NB,)),
            dma((NB,)),
            dma((NB,)),
            dma((NB,)),
        ],
        compiler_params=pltpu.CompilerParams(
            collective_id=0, has_side_effects=True, vmem_limit_bytes=48 * 2**20
        ),
    )(*[pltpu.with_memory_space_constraint(a, pltpu.HBM) for a in (lengths, q_nope, q_rope, w_uk, w_uv, cache_t)])


def solution(mesh):
    in_specs = (
        P("req", "kv", None),
        P("req", "kv", None),
        P("req", "kv", None),
        P("req"),
        P("kv", None, None),
        P("kv", None, None),
    )
    return jax.shard_map(
        local, mesh=mesh, in_specs=in_specs, out_specs=P("req", "kv"), check_vma=False
    )
```

```python
import functools
import math

import jax
import jax.numpy as jnp
from jax import lax
from jax.experimental import pallas as pl
from jax.experimental.pallas import tpu as pltpu
from jax.sharding import PartitionSpec as P

MESH = pl.DeviceIdType.MESH
F32 = jnp.float32
BF16 = jnp.bfloat16
NX, NZ = 4, 8
NB, NH = 4, 4
LANES = 128
DEAD = -1e30
CHUNK = 512


def to_lanes(column, rows):
    row = lax.broadcasted_iota(jnp.int32, (rows, LANES), 0)
    lane = lax.broadcasted_iota(jnp.int32, (rows, LANES), 1)
    return jnp.sum(jnp.where(row == lane, column, 0.0), axis=0, keepdims=True)


def to_column(row, picked):
    return jnp.sum(jnp.where(picked, row, 0.0), axis=1, keepdims=True)


def kernel(
    scale,
    lengths_hbm,
    q_nope_hbm,
    q_rope_hbm,
    w_uk_hbm,
    w_uv_hbm,
    cache_hbm,
    out,
    lengths,
    q_nope,
    q_rope,
    w_uk,
    w_uv,
    cache,
    natural,
    gathered,
    ropes,
    flat,
    rope_flat,
    query,
    scores,
    probs,
    x_send,
    x_recv,
    x_stat,
    turn,
    z_send,
    z_recv,
    z_stat,
    latent,
    local_sem,
    send_sem,
    gz_sem,
    gx_sem,
    rx_sem,
    rz_sem,
    rxs_sem,
    rzs_sem,
):
    req = lax.axis_index("req")
    kv = lax.axis_index("kv")
    z = lax.div(kv, NX)
    x = lax.rem(kv, NX)
    split_len = cache.shape[2]
    latent_width = w_uk.shape[2]
    z_order = (4, 3, 5, 2, 6, 1, 7)
    x_order = (2, 1, 3)

    def z_at(d):
        return lax.rem(z + d, NZ)

    def x_at(d):
        return lax.rem(x + d, NX)

    barrier = pltpu.get_barrier_semaphore()
    for d in z_order:
        pl.semaphore_signal(barrier, inc=1, device_id=(req, z_at(d) * NX + x), device_id_type=MESH)
    for d in x_order:
        pl.semaphore_signal(barrier, inc=1, device_id=(req, z * NX + x_at(d)), device_id_type=MESH)

    first_copies = [
        pltpu.make_async_copy(q_rope_hbm, q_rope, local_sem.at[6]),
        pltpu.make_async_copy(q_nope_hbm, q_nope, local_sem.at[7]),
        pltpu.make_async_copy(w_uk_hbm, w_uk, local_sem.at[4]),
    ]
    for copy in first_copies:
        copy.start()
    lengths_copy = pltpu.make_async_copy(lengths_hbm, lengths, local_sem.at[8])
    lengths_copy.start()

    def cache_copy(b):
        return pltpu.make_async_copy(cache_hbm.at[b], cache.at[b], local_sem.at[b])

    for b in range(NB):
        cache_copy(b).start()
    uv_copy = pltpu.make_async_copy(w_uv_hbm, w_uv, local_sem.at[5])
    uv_copy.start()

    def to_z(src, dst, kind, sem, d):
        return pltpu.make_async_remote_copy(
            src_ref=src,
            dst_ref=dst,
            send_sem=send_sem.at[kind],
            recv_sem=sem,
            device_id=(req, z_at(d) * NX + x),
            device_id_type=MESH,
        )

    def to_x(src, dst, kind, sem, d):
        return pltpu.make_async_remote_copy(
            src_ref=src,
            dst_ref=dst,
            send_sem=send_sem.at[kind],
            recv_sem=sem,
            device_id=(req, z * NX + x_at(d)),
            device_id_type=MESH,
        )

    def take(ref, sem):
        pltpu.make_async_copy(ref, ref, sem).wait()

    for copy in first_copies:
        copy.wait()
    for b in range(NB):
        flat[b * NH : (b + 1) * NH, :] = q_nope[b].astype(F32)
        rope = q_rope[b].astype(F32)
        for h in range(NH):
            r = b * 2 + h // 2
            rope_flat[r : r + 1, (h % 2) * 64 : (h % 2) * 64 + 64] = rope[h : h + 1, :]
    ropes[x, z] = rope_flat[0:8, :].astype(BF16)
    rows = flat[0:16, :]
    head = lax.rem(lax.broadcasted_iota(jnp.int32, (16, LANES), 0), NH)
    q_lat = jnp.zeros((16, latent_width), F32)
    for h in range(NH):
        own = jnp.where(head == h, rows, 0.0).astype(BF16)
        q_lat = q_lat + jnp.dot(own, w_uk[h], preferred_element_type=F32)
    for b in range(NB):
        for j in range(4):
            flat[b * 16 + j * NH : b * 16 + (j + 1) * NH, :] = q_lat[
                b * NH : (b + 1) * NH, j * LANES : (j + 1) * LANES
            ]
    for b in range(NB):
        gathered[b, x, z] = flat[b * 16 : (b + 1) * 16, :].astype(BF16)

    pl.semaphore_wait(barrier, NZ - 1 + NX - 1)

    for d in z_order:
        to_z(ropes.at[x, z], ropes.at[x, z], 1, gz_sem.at[NB], d).start()
    for b in range(NB):
        for d in z_order:
            to_z(gathered.at[b, x, z], gathered.at[b, x, z], 0, gz_sem.at[b], d).start()
    def turn_cache(b, carry):
        cache_copy(b).wait()
        for c in range(0, split_len, 256):
            natural[b, c : c + 256, :] = jnp.transpose(cache[b, 0:512, c : c + 256])
        return carry

    lax.fori_loop(0, NB, turn_cache, 0)

    take(ropes.at[0, pl.ds(0, NZ - 1)], gz_sem.at[NB])
    for d in x_order:
        to_x(ropes.at[x], ropes.at[x], 3, gx_sem.at[NB], d).start()
    def pass_on(b):
        take(gathered.at[b, 0, pl.ds(0, NZ - 1)], gz_sem.at[b])
        for d in x_order:
            to_x(gathered.at[b, x], gathered.at[b, x], 2, gx_sem.at[b], d).start()

    core = lax.rem(req, 2)
    for b in range(3):
        pass_on(b)

    @pl.when(core == 0)
    def _():
        for b in range(3, NB):
            pass_on(b)

    take(ropes.at[pl.ds(0, NX - 1)], gx_sem.at[NB])
    rope_flat[...] = ropes[...].reshape(NX * NZ * 8, LANES).astype(F32)

    lengths_copy.wait()
    position = kv * split_len + lax.broadcasted_iota(jnp.int32, (1, CHUNK), 1)

    def attend(b, carry):
        take(gathered.at[b, pl.ds(0, NX - 1)], gx_sem.at[b])
        flat[...] = gathered[b].reshape(NX * NZ * 16, LANES).astype(F32)
        for xs in range(NX):
            for hp in range(0, NH, 2):
                at = xs * 32 + hp * 8
                for j in range(4):
                    pair = [
                        flat[pl.ds(xs * 128 + j * NH + h, 8, stride=16), :] for h in (hp, hp + 1)
                    ]
                    query[at : at + 16, j * LANES : (j + 1) * LANES] = jnp.concatenate(
                        pair, axis=0
                    ).astype(BF16)
                both = rope_flat[pl.ds(xs * 64 + b * 2 + hp // 2, 8, stride=8), :]
                query[at : at + 16, 512:576] = jnp.concatenate(
                    [both[:, 0:64], both[:, 64:128]], axis=0
                ).astype(BF16)
        q = query[...]
        length = lengths[b]
        peak = None
        for c in range(0, split_len, CHUNK):
            s = jnp.dot(q, cache[b, :, c : c + CHUNK], preferred_element_type=F32)
            s = jnp.where(position + c < length, s, DEAD)
            scores[:, c : c + CHUNK] = s
            for k in range(0, CHUNK, LANES):
                piece = s[:, k : k + LANES]
                peak = piece if peak is None else jnp.maximum(peak, piece)
        top = jnp.max(peak, axis=1, keepdims=True) * scale
        total = jnp.zeros((128, LANES), F32)
        for c in range(0, split_len, CHUNK):
            p = jnp.exp2(scores[:, c : c + CHUNK] * scale - top)
            probs[:, c : c + CHUNK] = p.astype(BF16)
            for k in range(0, CHUNK, LANES):
                total = total + p[:, k : k + LANES]
        o = jnp.dot(probs[...], natural[b], preferred_element_type=F32)
        x_send[b] = o.astype(BF16)
        x_stat[b, x, 0:1, :] = to_lanes(top, 128)
        x_stat[b, x, 1:2, :] = to_lanes(jnp.sum(total, axis=1, keepdims=True), 128)
        for d in x_order:
            to_x(x_stat.at[b, x], x_stat.at[b, x], 5, rxs_sem.at[b], d).start()
            rows_there = pl.ds(pl.multiple_of(x_at(d) * 32, 32), 32)
            to_x(x_send.at[b, rows_there], x_recv.at[b, x], 4, rx_sem.at[b], d).start()

        @pl.when((core == 1) & (b + 3 < NB))
        def _():
            pass_on(b + 3)

        return carry

    lax.fori_loop(0, NB, attend, 0)

    def reduce_x(b, carry):
        take(x_stat.at[b, pl.ds(0, NX - 1)], rxs_sem.at[b])
        take(x_recv.at[b, pl.ds(0, NX - 1)], rx_sem.at[b])
        row = lax.broadcasted_iota(jnp.int32, (32, LANES), 0)
        lane = lax.broadcasted_iota(jnp.int32, (32, LANES), 1)
        picked = lane == row + x * 32
        tops, sums = [], []
        for d in (0,) + x_order:
            stat = x_stat[b, x_at(d)]
            tops.append(to_column(stat[0:1, :], picked))
            sums.append(to_column(stat[1:2, :], picked))
        top = functools.reduce(jnp.maximum, tops)
        weights = [jnp.exp2(t - top) for t in tops]
        total = sum(w * s for w, s in zip(weights, sums))
        z_stat[b, z, 0:1, :] = to_lanes(top, 32)
        z_stat[b, z, 1:2, :] = to_lanes(total, 32)
        acc = x_send[b, pl.ds(pl.multiple_of(x * 32, 32), 32), :].astype(F32) * weights[0]
        for d, w in zip(x_order, weights[1:]):
            acc = acc + x_recv[b, x_at(d)].astype(F32) * w
        for h in range(NH):
            for j in range(4):
                r = h * 4 + j
                turn[r * 8 : r * 8 + 8, :] = acc[h * 8 : h * 8 + 8, j * LANES : (j + 1) * LANES]
        for zs in range(NZ):
            z_send[b, zs] = turn[pl.ds(zs, 16, stride=8), :].astype(BF16)
        for d in z_order:
            to_z(z_stat.at[b, z], z_stat.at[b, z], 7, rzs_sem.at[b], d).start()
            to_z(z_send.at[b, z_at(d)], z_recv.at[b, z], 6, rz_sem.at[b], d).start()
        return carry

    lax.fori_loop(0, NB, reduce_x, 0)

    def reduce_z(b, carry):
        take(z_stat.at[b, pl.ds(0, NZ - 1)], rzs_sem.at[b])
        take(z_recv.at[b, pl.ds(0, NZ - 1)], rz_sem.at[b])
        row = lax.broadcasted_iota(jnp.int32, (16, LANES), 0)
        lane = lax.broadcasted_iota(jnp.int32, (16, LANES), 1)
        picked = lane == lax.div(row, 4) * 8 + z
        tops, sums = [], []
        for d in (0,) + z_order:
            stat = z_stat[b, z_at(d)]
            tops.append(to_column(stat[0:1, :], picked))
            sums.append(to_column(stat[1:2, :], picked))
        top = functools.reduce(jnp.maximum, tops)
        weights = [jnp.exp2(t - top) for t in tops]
        total = sum(w * s for w, s in zip(weights, sums))
        acc = z_send[b, z].astype(F32) * weights[0]
        for d, w in zip(z_order, weights[1:]):
            acc = acc + z_recv[b, z_at(d)].astype(F32) * w
        latent[pl.ds(pl.multiple_of(b * 16, 16), 16), :] = acc / total
        return carry

    lax.fori_loop(0, NB, reduce_z, 0)

    uv_copy.wait()
    for h in range(NH):
        lat = jnp.concatenate(
            [latent[pl.ds(h * 4 + j, NB, stride=16), :] for j in range(4)], axis=1
        ).astype(BF16)
        out[:, h * LANES : (h + 1) * LANES] = jnp.dot(
            lat, w_uv[h], preferred_element_type=F32
        ).astype(BF16)

    take(gathered.at[pl.ds(0, NB), 0, pl.ds(0, NZ - 1)], send_sem.at[0])
    take(ropes.at[0, pl.ds(0, NZ - 1)], send_sem.at[1])
    take(gathered.at[pl.ds(0, NB), pl.ds(0, NX - 1)], send_sem.at[2])
    take(ropes.at[pl.ds(0, NX - 1)], send_sem.at[3])
    take(x_recv.at[pl.ds(0, NB), pl.ds(0, NX - 1)], send_sem.at[4])
    take(x_stat.at[pl.ds(0, NB), pl.ds(0, NX - 1)], send_sem.at[5])
    take(z_recv.at[pl.ds(0, NB), pl.ds(0, NZ - 1)], send_sem.at[6])
    take(z_stat.at[pl.ds(0, NB), pl.ds(0, NZ - 1)], send_sem.at[7])


def local(q_nope, q_rope, cache, lengths, w_uk, w_uv):
    scale = (q_nope.shape[2] + q_rope.shape[2]) ** (-0.5) * math.log2(math.e)
    cache_t = jnp.swapaxes(cache, 1, 2)
    vmem = pl.BlockSpec(memory_space=pltpu.VMEM)
    hbm = pl.BlockSpec(memory_space=pl.ANY)
    dma = pltpu.SemaphoreType.DMA
    return pl.pallas_call(
        functools.partial(kernel, scale),
        out_shape=jax.ShapeDtypeStruct((NB, NH * w_uv.shape[2]), BF16),
        in_specs=[hbm] * 6,
        out_specs=vmem,
        scratch_shapes=[
            pltpu.SMEM(lengths.shape, jnp.int32),
            pltpu.VMEM(q_nope.shape, BF16),
            pltpu.VMEM(q_rope.shape, BF16),
            pltpu.VMEM(w_uk.shape, BF16),
            pltpu.VMEM(w_uv.shape, BF16),
            pltpu.VMEM(cache_t.shape, BF16),
            pltpu.VMEM((NB, cache_t.shape[2], 512), BF16),
            pltpu.VMEM((NB, NX, NZ, 16, LANES), BF16),
            pltpu.VMEM((NX, NZ, 8, LANES), BF16),
            pltpu.VMEM((NX * NZ * 16, LANES), F32),
            pltpu.VMEM((NX * NZ * 8, LANES), F32),
            pltpu.VMEM((128, 576), BF16),
            pltpu.VMEM((128, cache_t.shape[2]), F32),
            pltpu.VMEM((128, cache_t.shape[2]), BF16),
            pltpu.VMEM((NB, 128, 512), BF16),
            pltpu.VMEM((NB, NX, 32, 512), BF16),
            pltpu.VMEM((NB, NX, 2, LANES), F32),
            pltpu.VMEM((128, LANES), F32),
            pltpu.VMEM((NB, NZ, 16, LANES), BF16),
            pltpu.VMEM((NB, NZ, 16, LANES), BF16),
            pltpu.VMEM((NB, NZ, 2, LANES), F32),
            pltpu.VMEM((NB * 16, LANES), F32),
            dma((9,)),
            dma((8,)),
            dma((NB + 1,)),
            dma((NB + 1,)),
            dma((NB,)),
            dma((NB,)),
            dma((NB,)),
            dma((NB,)),
        ],
        compiler_params=pltpu.CompilerParams(
            collective_id=0, has_side_effects=True, vmem_limit_bytes=48 * 2**20
        ),
    )(*[pltpu.with_memory_space_constraint(a, pltpu.HBM) for a in (lengths, q_nope, q_rope, w_uk, w_uv, cache_t)])


def solution(mesh):
    in_specs = (
        P("req", "kv", None),
        P("req", "kv", None),
        P("req", "kv", None),
        P("req"),
        P("kv", None, None),
        P("kv", None, None),
    )
    return jax.shard_map(
        local, mesh=mesh, in_specs=in_specs, out_specs=P("req", "kv"), check_vma=False
    )
```

```python
import functools
import math

import jax
import jax.numpy as jnp
from jax import lax
from jax.experimental import pallas as pl
from jax.experimental.pallas import tpu as pltpu
from jax.sharding import PartitionSpec as P

MESH = pl.DeviceIdType.MESH
F32 = jnp.float32
BF16 = jnp.bfloat16
NX, NZ = 4, 8
NB, NH = 4, 4
LANES = 128
DEAD = -1e30
CHUNK = 512


def to_lanes(column, rows):
    row = lax.broadcasted_iota(jnp.int32, (rows, LANES), 0)
    lane = lax.broadcasted_iota(jnp.int32, (rows, LANES), 1)
    return jnp.sum(jnp.where(row == lane, column, 0.0), axis=0, keepdims=True)


def to_column(row, picked):
    return jnp.sum(jnp.where(picked, row, 0.0), axis=1, keepdims=True)


def kernel(
    scale,
    lengths_hbm,
    q_nope_hbm,
    q_rope_hbm,
    w_uk_hbm,
    w_uv_hbm,
    cache_hbm,
    out,
    lengths,
    q_nope,
    q_rope,
    w_uk,
    w_uv,
    cache,
    natural,
    gathered,
    ropes,
    flat,
    rope_flat,
    query,
    scores,
    probs,
    x_send,
    x_recv,
    x_stat,
    turn,
    z_send,
    z_recv,
    z_stat,
    latent,
    local_sem,
    send_sem,
    gz_sem,
    gx_sem,
    rx_sem,
    rz_sem,
    rxs_sem,
    rzs_sem,
):
    req = lax.axis_index("req")
    kv = lax.axis_index("kv")
    z = lax.div(kv, NX)
    x = lax.rem(kv, NX)
    split_len = cache.shape[2]
    latent_width = w_uk.shape[2]
    z_order = (4, 3, 5, 2, 6, 1, 7)
    x_order = (2, 1, 3)

    def z_at(d):
        return lax.rem(z + d, NZ)

    def x_at(d):
        return lax.rem(x + d, NX)

    barrier = pltpu.get_barrier_semaphore()
    for d in z_order:
        pl.semaphore_signal(barrier, inc=1, device_id=(req, z_at(d) * NX + x), device_id_type=MESH)
    for d in x_order:
        pl.semaphore_signal(barrier, inc=1, device_id=(req, z * NX + x_at(d)), device_id_type=MESH)

    first_copies = [
        pltpu.make_async_copy(q_rope_hbm, q_rope, local_sem.at[6]),
        pltpu.make_async_copy(q_nope_hbm, q_nope, local_sem.at[7]),
        pltpu.make_async_copy(w_uk_hbm, w_uk, local_sem.at[4]),
    ]
    for copy in first_copies:
        copy.start()
    lengths_copy = pltpu.make_async_copy(lengths_hbm, lengths, local_sem.at[8])
    lengths_copy.start()

    def cache_copy(b):
        return pltpu.make_async_copy(cache_hbm.at[b], cache.at[b], local_sem.at[b])

    for b in range(NB):
        cache_copy(b).start()
    uv_copy = pltpu.make_async_copy(w_uv_hbm, w_uv, local_sem.at[5])
    uv_copy.start()

    def to_z(src, dst, kind, sem, d):
        return pltpu.make_async_remote_copy(
            src_ref=src,
            dst_ref=dst,
            send_sem=send_sem.at[kind],
            recv_sem=sem,
            device_id=(req, z_at(d) * NX + x),
            device_id_type=MESH,
        )

    def to_x(src, dst, kind, sem, d):
        return pltpu.make_async_remote_copy(
            src_ref=src,
            dst_ref=dst,
            send_sem=send_sem.at[kind],
            recv_sem=sem,
            device_id=(req, z * NX + x_at(d)),
            device_id_type=MESH,
        )

    def take(ref, sem):
        pltpu.make_async_copy(ref, ref, sem).wait()

    for copy in first_copies:
        copy.wait()
    for b in range(NB):
        flat[b * NH : (b + 1) * NH, :] = q_nope[b].astype(F32)
        rope = q_rope[b].astype(F32)
        for h in range(NH):
            r = b * 2 + h // 2
            rope_flat[r : r + 1, (h % 2) * 64 : (h % 2) * 64 + 64] = rope[h : h + 1, :]
    ropes[z, x] = rope_flat[0:8, :].astype(BF16)
    rows = flat[0:16, :]
    head = lax.rem(lax.broadcasted_iota(jnp.int32, (16, LANES), 0), NH)
    q_lat = jnp.zeros((16, latent_width), F32)
    for h in range(NH):
        own = jnp.where(head == h, rows, 0.0).astype(BF16)
        q_lat = q_lat + jnp.dot(own, w_uk[h], preferred_element_type=F32)
    for b in range(NB):
        for j in range(4):
            flat[b * 16 + j * NH : b * 16 + (j + 1) * NH, :] = q_lat[
                b * NH : (b + 1) * NH, j * LANES : (j + 1) * LANES
            ]
    for b in range(NB):
        gathered[b, x, z] = flat[b * 16 : (b + 1) * 16, :].astype(BF16)

    pl.semaphore_wait(barrier, NZ - 1 + NX - 1)

    for d in x_order:
        to_x(ropes.at[z, x], ropes.at[z, x], 3, gx_sem.at[NB], d).start()
    for b in range(NB):
        for d in z_order:
            to_z(gathered.at[b, x, z], gathered.at[b, x, z], 0, gz_sem.at[b], d).start()
    def turn_cache(b, carry):
        cache_copy(b).wait()
        for c in range(0, split_len, 256):
            natural[b, c : c + 256, :] = jnp.transpose(cache[b, 0:512, c : c + 256])
        return carry

    lax.fori_loop(0, NB - 1, turn_cache, 0)

    take(ropes.at[0, pl.ds(0, NX - 1)], gx_sem.at[NB])
    for d in z_order:
        to_z(ropes.at[z], ropes.at[z], 1, gz_sem.at[NB], d).start()
    turn_cache(NB - 1, 0)
    def pass_on(b):
        take(gathered.at[b, 0, pl.ds(0, NZ - 1)], gz_sem.at[b])
        for d in x_order:
            to_x(gathered.at[b, x], gathered.at[b, x], 2, gx_sem.at[b], d).start()

    core = lax.rem(req, 2)
    for b in range(3):
        pass_on(b)

    @pl.when(core == 0)
    def _():
        for b in range(3, NB):
            pass_on(b)

    take(ropes.at[pl.ds(0, NZ - 1)], gz_sem.at[NB])
    rope_flat[...] = ropes[...].reshape(NX * NZ * 8, LANES).astype(F32)

    lengths_copy.wait()
    position = kv * split_len + lax.broadcasted_iota(jnp.int32, (1, CHUNK), 1)

    def attend(b, carry):
        take(gathered.at[b, pl.ds(0, NX - 1)], gx_sem.at[b])
        flat[...] = gathered[b].reshape(NX * NZ * 16, LANES).astype(F32)
        for xs in range(NX):
            for hp in range(0, NH, 2):
                at = xs * 32 + hp * 8
                for j in range(4):
                    pair = [
                        flat[pl.ds(xs * 128 + j * NH + h, 8, stride=16), :] for h in (hp, hp + 1)
                    ]
                    query[at : at + 16, j * LANES : (j + 1) * LANES] = jnp.concatenate(
                        pair, axis=0
                    ).astype(BF16)
                both = rope_flat[pl.ds(xs * 8 + b * 2 + hp // 2, 8, stride=32), :]
                query[at : at + 16, 512:576] = jnp.concatenate(
                    [both[:, 0:64], both[:, 64:128]], axis=0
                ).astype(BF16)
        q = query[...]
        length = lengths[b]
        peak = None
        for c in range(0, split_len, CHUNK):
            s = jnp.dot(q, cache[b, :, c : c + CHUNK], preferred_element_type=F32)
            s = jnp.where(position + c < length, s, DEAD)
            scores[:, c : c + CHUNK] = s
            for k in range(0, CHUNK, LANES):
                piece = s[:, k : k + LANES]
                peak = piece if peak is None else jnp.maximum(peak, piece)
        top = jnp.max(peak, axis=1, keepdims=True) * scale
        total = jnp.zeros((128, LANES), F32)
        for c in range(0, split_len, CHUNK):
            p = jnp.exp2(scores[:, c : c + CHUNK] * scale - top)
            probs[:, c : c + CHUNK] = p.astype(BF16)
            for k in range(0, CHUNK, LANES):
                total = total + p[:, k : k + LANES]
        o = jnp.dot(probs[...], natural[b], preferred_element_type=F32)
        x_send[b] = o.astype(BF16)
        x_stat[b, x, 0:1, :] = to_lanes(top, 128)
        x_stat[b, x, 1:2, :] = to_lanes(jnp.sum(total, axis=1, keepdims=True), 128)
        for d in x_order:
            to_x(x_stat.at[b, x], x_stat.at[b, x], 5, rxs_sem.at[b], d).start()
            rows_there = pl.ds(pl.multiple_of(x_at(d) * 32, 32), 32)
            to_x(x_send.at[b, rows_there], x_recv.at[b, x], 4, rx_sem.at[b], d).start()

        @pl.when((core == 1) & (b + 3 < NB))
        def _():
            pass_on(b + 3)

        return carry

    lax.fori_loop(0, NB, attend, 0)

    def reduce_x(b, carry):
        take(x_stat.at[b, pl.ds(0, NX - 1)], rxs_sem.at[b])
        take(x_recv.at[b, pl.ds(0, NX - 1)], rx_sem.at[b])
        row = lax.broadcasted_iota(jnp.int32, (32, LANES), 0)
        lane = lax.broadcasted_iota(jnp.int32, (32, LANES), 1)
        picked = lane == row + x * 32
        tops, sums = [], []
        for d in (0,) + x_order:
            stat = x_stat[b, x_at(d)]
            tops.append(to_column(stat[0:1, :], picked))
            sums.append(to_column(stat[1:2, :], picked))
        top = functools.reduce(jnp.maximum, tops)
        weights = [jnp.exp2(t - top) for t in tops]
        total = sum(w * s for w, s in zip(weights, sums))
        z_stat[b, z, 0:1, :] = to_lanes(top, 32)
        z_stat[b, z, 1:2, :] = to_lanes(total, 32)
        acc = x_send[b, pl.ds(pl.multiple_of(x * 32, 32), 32), :].astype(F32) * weights[0]
        for d, w in zip(x_order, weights[1:]):
            acc = acc + x_recv[b, x_at(d)].astype(F32) * w
        for h in range(NH):
            for j in range(4):
                r = h * 4 + j
                turn[r * 8 : r * 8 + 8, :] = acc[h * 8 : h * 8 + 8, j * LANES : (j + 1) * LANES]
        for zs in range(NZ):
            z_send[b, zs] = turn[pl.ds(zs, 16, stride=8), :].astype(BF16)
        for d in z_order:
            to_z(z_stat.at[b, z], z_stat.at[b, z], 7, rzs_sem.at[b], d).start()
            to_z(z_send.at[b, z_at(d)], z_recv.at[b, z], 6, rz_sem.at[b], d).start()
        return carry

    lax.fori_loop(0, NB, reduce_x, 0)

    def reduce_z(b, carry):
        take(z_stat.at[b, pl.ds(0, NZ - 1)], rzs_sem.at[b])
        take(z_recv.at[b, pl.ds(0, NZ - 1)], rz_sem.at[b])
        row = lax.broadcasted_iota(jnp.int32, (16, LANES), 0)
        lane = lax.broadcasted_iota(jnp.int32, (16, LANES), 1)
        picked = lane == lax.div(row, 4) * 8 + z
        tops, sums = [], []
        for d in (0,) + z_order:
            stat = z_stat[b, z_at(d)]
            tops.append(to_column(stat[0:1, :], picked))
            sums.append(to_column(stat[1:2, :], picked))
        top = functools.reduce(jnp.maximum, tops)
        weights = [jnp.exp2(t - top) for t in tops]
        total = sum(w * s for w, s in zip(weights, sums))
        acc = z_send[b, z].astype(F32) * weights[0]
        for d, w in zip(z_order, weights[1:]):
            acc = acc + z_recv[b, z_at(d)].astype(F32) * w
        latent[pl.ds(pl.multiple_of(b * 16, 16), 16), :] = acc / total
        return carry

    lax.fori_loop(0, NB, reduce_z, 0)

    uv_copy.wait()
    for h in range(NH):
        lat = jnp.concatenate(
            [latent[pl.ds(h * 4 + j, NB, stride=16), :] for j in range(4)], axis=1
        ).astype(BF16)
        out[:, h * LANES : (h + 1) * LANES] = jnp.dot(
            lat, w_uv[h], preferred_element_type=F32
        ).astype(BF16)

    take(gathered.at[pl.ds(0, NB), 0, pl.ds(0, NZ - 1)], send_sem.at[0])
    take(ropes.at[pl.ds(0, NZ - 1)], send_sem.at[1])
    take(gathered.at[pl.ds(0, NB), pl.ds(0, NX - 1)], send_sem.at[2])
    take(ropes.at[0, pl.ds(0, NX - 1)], send_sem.at[3])
    take(x_recv.at[pl.ds(0, NB), pl.ds(0, NX - 1)], send_sem.at[4])
    take(x_stat.at[pl.ds(0, NB), pl.ds(0, NX - 1)], send_sem.at[5])
    take(z_recv.at[pl.ds(0, NB), pl.ds(0, NZ - 1)], send_sem.at[6])
    take(z_stat.at[pl.ds(0, NB), pl.ds(0, NZ - 1)], send_sem.at[7])


def local(q_nope, q_rope, cache, lengths, w_uk, w_uv):
    scale = (q_nope.shape[2] + q_rope.shape[2]) ** (-0.5) * math.log2(math.e)
    cache_t = jnp.swapaxes(cache, 1, 2)
    vmem = pl.BlockSpec(memory_space=pltpu.VMEM)
    hbm = pl.BlockSpec(memory_space=pl.ANY)
    dma = pltpu.SemaphoreType.DMA
    return pl.pallas_call(
        functools.partial(kernel, scale),
        out_shape=jax.ShapeDtypeStruct((NB, NH * w_uv.shape[2]), BF16),
        in_specs=[hbm] * 6,
        out_specs=vmem,
        scratch_shapes=[
            pltpu.SMEM(lengths.shape, jnp.int32),
            pltpu.VMEM(q_nope.shape, BF16),
            pltpu.VMEM(q_rope.shape, BF16),
            pltpu.VMEM(w_uk.shape, BF16),
            pltpu.VMEM(w_uv.shape, BF16),
            pltpu.VMEM(cache_t.shape, BF16),
            pltpu.VMEM((NB, cache_t.shape[2], 512), BF16),
            pltpu.VMEM((NB, NX, NZ, 16, LANES), BF16),
            pltpu.VMEM((NZ, NX, 8, LANES), BF16),
            pltpu.VMEM((NX * NZ * 16, LANES), F32),
            pltpu.VMEM((NX * NZ * 8, LANES), F32),
            pltpu.VMEM((128, 576), BF16),
            pltpu.VMEM((128, cache_t.shape[2]), F32),
            pltpu.VMEM((128, cache_t.shape[2]), BF16),
            pltpu.VMEM((NB, 128, 512), BF16),
            pltpu.VMEM((NB, NX, 32, 512), BF16),
            pltpu.VMEM((NB, NX, 2, LANES), F32),
            pltpu.VMEM((128, LANES), F32),
            pltpu.VMEM((NB, NZ, 16, LANES), BF16),
            pltpu.VMEM((NB, NZ, 16, LANES), BF16),
            pltpu.VMEM((NB, NZ, 2, LANES), F32),
            pltpu.VMEM((NB * 16, LANES), F32),
            dma((9,)),
            dma((8,)),
            dma((NB + 1,)),
            dma((NB + 1,)),
            dma((NB,)),
            dma((NB,)),
            dma((NB,)),
            dma((NB,)),
        ],
        compiler_params=pltpu.CompilerParams(
            collective_id=0, has_side_effects=True, vmem_limit_bytes=48 * 2**20
        ),
    )(*[pltpu.with_memory_space_constraint(a, pltpu.HBM) for a in (lengths, q_nope, q_rope, w_uk, w_uv, cache_t)])


def solution(mesh):
    in_specs = (
        P("req", "kv", None),
        P("req", "kv", None),
        P("req", "kv", None),
        P("req"),
        P("kv", None, None),
        P("kv", None, None),
    )
    return jax.shard_map(
        local, mesh=mesh, in_specs=in_specs, out_specs=P("req", "kv"), check_vma=False
    )
```

```python
import functools
import math

import jax
import jax.numpy as jnp
from jax import lax
from jax.experimental import pallas as pl
from jax.experimental.pallas import tpu as pltpu
from jax.sharding import PartitionSpec as P

MESH = pl.DeviceIdType.MESH
F32 = jnp.float32
BF16 = jnp.bfloat16
NX, NZ = 4, 8
NB, NH = 4, 4
LANES = 128
DEAD = -1e30
CHUNK = 512


def to_lanes(column, rows):
    row = lax.broadcasted_iota(jnp.int32, (rows, LANES), 0)
    lane = lax.broadcasted_iota(jnp.int32, (rows, LANES), 1)
    return jnp.sum(jnp.where(row == lane, column, 0.0), axis=0, keepdims=True)


def to_column(row, picked):
    return jnp.sum(jnp.where(picked, row, 0.0), axis=1, keepdims=True)


def kernel(
    scale,
    lengths_hbm,
    q_nope_hbm,
    q_rope_hbm,
    w_uk_hbm,
    w_uv_hbm,
    cache_hbm,
    out,
    lengths,
    q_nope,
    q_rope,
    w_uk,
    w_uv,
    cache,
    natural,
    gathered,
    ropes,
    flat,
    rope_flat,
    query,
    scores,
    probs,
    x_send,
    x_recv,
    x_stat,
    turn,
    z_send,
    z_recv,
    z_stat,
    latent,
    local_sem,
    send_sem,
    gz_sem,
    gx_sem,
    rx_sem,
    rz_sem,
    rxs_sem,
    rzs_sem,
):
    req = lax.axis_index("req")
    kv = lax.axis_index("kv")
    z = lax.div(kv, NX)
    x = lax.rem(kv, NX)
    split_len = cache.shape[2]
    latent_width = w_uk.shape[2]
    z_order = (4, 3, 5, 2, 6, 1, 7)
    x_order = (2, 1, 3)

    def z_at(d):
        return lax.rem(z + d, NZ)

    def x_at(d):
        return lax.rem(x + d, NX)

    barrier = pltpu.get_barrier_semaphore()
    for d in z_order:
        pl.semaphore_signal(barrier, inc=1, device_id=(req, z_at(d) * NX + x), device_id_type=MESH)
    for d in x_order:
        pl.semaphore_signal(barrier, inc=1, device_id=(req, z * NX + x_at(d)), device_id_type=MESH)

    first_copies = [
        pltpu.make_async_copy(q_rope_hbm, q_rope, local_sem.at[6]),
        pltpu.make_async_copy(q_nope_hbm, q_nope, local_sem.at[7]),
        pltpu.make_async_copy(w_uk_hbm, w_uk, local_sem.at[4]),
    ]
    for copy in first_copies:
        copy.start()
    lengths_copy = pltpu.make_async_copy(lengths_hbm, lengths, local_sem.at[8])
    lengths_copy.start()

    def cache_copy(b):
        return pltpu.make_async_copy(cache_hbm.at[b], cache.at[b], local_sem.at[b])

    for b in range(NB):
        cache_copy(b).start()
    uv_copy = pltpu.make_async_copy(w_uv_hbm, w_uv, local_sem.at[5])
    uv_copy.start()

    def to_z(src, dst, kind, sem, d):
        return pltpu.make_async_remote_copy(
            src_ref=src,
            dst_ref=dst,
            send_sem=send_sem.at[kind],
            recv_sem=sem,
            device_id=(req, z_at(d) * NX + x),
            device_id_type=MESH,
        )

    def to_x(src, dst, kind, sem, d):
        return pltpu.make_async_remote_copy(
            src_ref=src,
            dst_ref=dst,
            send_sem=send_sem.at[kind],
            recv_sem=sem,
            device_id=(req, z * NX + x_at(d)),
            device_id_type=MESH,
        )

    def take(ref, sem):
        pltpu.make_async_copy(ref, ref, sem).wait()

    for copy in first_copies:
        copy.wait()
    for b in range(NB):
        flat[b * NH : (b + 1) * NH, :] = q_nope[b].astype(F32)
        rope = q_rope[b].astype(F32)
        for h in range(NH):
            r = b * 2 + h // 2
            rope_flat[r : r + 1, (h % 2) * 64 : (h % 2) * 64 + 64] = rope[h : h + 1, :]
    ropes[z, x] = rope_flat[0:8, :].astype(BF16)
    rows = flat[0:16, :]
    head = lax.rem(lax.broadcasted_iota(jnp.int32, (16, LANES), 0), NH)
    q_lat = jnp.zeros((16, latent_width), F32)
    for h in range(NH):
        own = jnp.where(head == h, rows, 0.0).astype(BF16)
        q_lat = q_lat + jnp.dot(own, w_uk[h], preferred_element_type=F32)
    for b in range(NB):
        for j in range(4):
            flat[b * 16 + j * NH : b * 16 + (j + 1) * NH, :] = q_lat[
                b * NH : (b + 1) * NH, j * LANES : (j + 1) * LANES
            ]
    for b in range(NB):
        gathered[b, x, z] = flat[b * 16 : (b + 1) * 16, :].astype(BF16)

    pl.semaphore_wait(barrier, NZ - 1 + NX - 1)

    for d in x_order:
        to_x(ropes.at[z, x], ropes.at[z, x], 3, gx_sem.at[NB], d).start()
    for b in range(NB):
        for d in z_order:
            to_z(gathered.at[b, x, z], gathered.at[b, x, z], 0, gz_sem.at[b], d).start()
    def turn_cache(b, carry):
        cache_copy(b).wait()
        for c in range(0, split_len, 256):
            natural[b, c : c + 256, :] = jnp.transpose(cache[b, 0:512, c : c + 256])
        return carry

    lax.fori_loop(0, NB - 1, turn_cache, 0)

    take(ropes.at[0, pl.ds(0, NX - 1)], gx_sem.at[NB])
    for d in z_order:
        to_z(ropes.at[z], ropes.at[z], 1, gz_sem.at[NB], d).start()
    turn_cache(NB - 1, 0)
    def pass_on(b):
        take(gathered.at[b, 0, pl.ds(0, NZ - 1)], gz_sem.at[b])
        for d in x_order:
            to_x(gathered.at[b, x], gathered.at[b, x], 2, gx_sem.at[b], d).start()

    core = lax.rem(req, 2)
    for b in range(3):
        pass_on(b)

    @pl.when(core == 0)
    def _():
        for b in range(3, NB):
            pass_on(b)

    take(ropes.at[pl.ds(0, NZ - 1)], gz_sem.at[NB])
    rope_flat[...] = ropes[...].reshape(NX * NZ * 8, LANES).astype(F32)

    lengths_copy.wait()
    position = kv * split_len + lax.broadcasted_iota(jnp.int32, (1, CHUNK), 1)

    def attend(b, carry):
        take(gathered.at[b, pl.ds(0, NX - 1)], gx_sem.at[b])
        flat[...] = gathered[b].reshape(NX * NZ * 16, LANES).astype(F32)
        for xs in range(NX):
            for hp in range(0, NH, 2):
                at = xs * 32 + hp * 8
                for j in range(4):
                    pair = [
                        flat[pl.ds(xs * 128 + j * NH + h, 8, stride=16), :] for h in (hp, hp + 1)
                    ]
                    query[at : at + 16, j * LANES : (j + 1) * LANES] = jnp.concatenate(
                        pair, axis=0
                    ).astype(BF16)
                both = rope_flat[pl.ds(xs * 8 + b * 2 + hp // 2, 8, stride=32), :]
                query[at : at + 16, 512:576] = jnp.concatenate(
                    [both[:, 0:64], both[:, 64:128]], axis=0
                ).astype(BF16)
        q = query[...]
        length = lengths[b]
        peak = None
        for c in range(0, split_len, CHUNK):
            s = jnp.dot(q, cache[b, :, c : c + CHUNK], preferred_element_type=F32)
            s = jnp.where(position + c < length, s, DEAD)
            scores[:, c : c + CHUNK] = s
            for k in range(0, CHUNK, LANES):
                piece = s[:, k : k + LANES]
                peak = piece if peak is None else jnp.maximum(peak, piece)
        top = jnp.max(peak, axis=1, keepdims=True) * scale
        total = jnp.zeros((128, LANES), F32)
        for c in range(0, split_len, CHUNK):
            p = jnp.exp2(scores[:, c : c + CHUNK] * scale - top)
            probs[:, c : c + CHUNK] = p.astype(BF16)
            for k in range(0, CHUNK, LANES):
                total = total + p[:, k : k + LANES]
        o = jnp.dot(probs[...], natural[b], preferred_element_type=F32)
        x_send[b] = o.astype(BF16)
        x_stat[b, x, 0:1, :] = to_lanes(top, 128)
        x_stat[b, x, 1:2, :] = to_lanes(jnp.sum(total, axis=1, keepdims=True), 128)
        for d in x_order:
            to_x(x_stat.at[b, x], x_stat.at[b, x], 5, rxs_sem.at[b], d).start()
            rows_there = pl.ds(pl.multiple_of(x_at(d) * 32, 32), 32)
            to_x(x_send.at[b, rows_there], x_recv.at[b, x], 4, rx_sem.at[b], d).start()

        @pl.when((core == 1) & (b + 3 < NB))
        def _():
            pass_on(b + 3)

        return carry

    lax.fori_loop(0, NB, attend, 0)

    def reduce_x(b, carry):
        take(x_stat.at[b, pl.ds(0, NX - 1)], rxs_sem.at[b])
        take(x_recv.at[b, pl.ds(0, NX - 1)], rx_sem.at[b])
        row = lax.broadcasted_iota(jnp.int32, (32, LANES), 0)
        lane = lax.broadcasted_iota(jnp.int32, (32, LANES), 1)
        picked = lane == row + x * 32
        tops, sums = [], []
        for d in (0,) + x_order:
            stat = x_stat[b, x_at(d)]
            tops.append(to_column(stat[0:1, :], picked))
            sums.append(to_column(stat[1:2, :], picked))
        top = functools.reduce(jnp.maximum, tops)
        weights = [jnp.exp2(t - top) for t in tops]
        total = sum(w * s for w, s in zip(weights, sums))
        z_stat[b, z, 0:1, :] = to_lanes(top, 32)
        z_stat[b, z, 1:2, :] = to_lanes(total, 32)
        acc = x_send[b, pl.ds(pl.multiple_of(x * 32, 32), 32), :].astype(F32) * weights[0]
        for d, w in zip(x_order, weights[1:]):
            acc = acc + x_recv[b, x_at(d)].astype(F32) * w
        for h in range(NH):
            for j in range(4):
                r = h * 4 + j
                turn[r * 8 : r * 8 + 8, :] = acc[h * 8 : h * 8 + 8, j * LANES : (j + 1) * LANES]
        for zs in range(NZ):
            z_send[b, zs] = turn[pl.ds(zs, 16, stride=8), :].astype(BF16)
        for d in z_order:
            to_z(z_stat.at[b, z], z_stat.at[b, z], 7, rzs_sem.at[b], d).start()
            to_z(z_send.at[b, z_at(d)], z_recv.at[b, z], 6, rz_sem.at[b], d).start()
        return carry

    lax.fori_loop(0, NB, reduce_x, 0)

    def reduce_z(b, carry):
        take(z_stat.at[b, pl.ds(0, NZ - 1)], rzs_sem.at[b])
        take(z_recv.at[b, pl.ds(0, NZ - 1)], rz_sem.at[b])
        row = lax.broadcasted_iota(jnp.int32, (16, LANES), 0)
        lane = lax.broadcasted_iota(jnp.int32, (16, LANES), 1)
        picked = lane == lax.div(row, 4) * 8 + z
        tops, sums = [], []
        for d in (0,) + z_order:
            stat = z_stat[b, z_at(d)]
            tops.append(to_column(stat[0:1, :], picked))
            sums.append(to_column(stat[1:2, :], picked))
        top = functools.reduce(jnp.maximum, tops)
        weights = [jnp.exp2(t - top) for t in tops]
        total = sum(w * s for w, s in zip(weights, sums))
        acc = z_send[b, z].astype(F32) * weights[0]
        for d, w in zip(z_order, weights[1:]):
            acc = acc + z_recv[b, z_at(d)].astype(F32) * w
        latent[pl.ds(pl.multiple_of(b * 16, 16), 16), :] = acc / total
        return carry

    lax.fori_loop(0, NB, reduce_z, 0, unroll=True)

    uv_copy.wait()
    for h in range(NH):
        lat = jnp.concatenate(
            [latent[pl.ds(h * 4 + j, NB, stride=16), :] for j in range(4)], axis=1
        ).astype(BF16)
        out[:, h * LANES : (h + 1) * LANES] = jnp.dot(
            lat, w_uv[h], preferred_element_type=F32
        ).astype(BF16)

    take(gathered.at[pl.ds(0, NB), 0, pl.ds(0, NZ - 1)], send_sem.at[0])
    take(ropes.at[pl.ds(0, NZ - 1)], send_sem.at[1])
    take(gathered.at[pl.ds(0, NB), pl.ds(0, NX - 1)], send_sem.at[2])
    take(ropes.at[0, pl.ds(0, NX - 1)], send_sem.at[3])
    take(x_recv.at[pl.ds(0, NB), pl.ds(0, NX - 1)], send_sem.at[4])
    take(x_stat.at[pl.ds(0, NB), pl.ds(0, NX - 1)], send_sem.at[5])
    take(z_recv.at[pl.ds(0, NB), pl.ds(0, NZ - 1)], send_sem.at[6])
    take(z_stat.at[pl.ds(0, NB), pl.ds(0, NZ - 1)], send_sem.at[7])


def local(q_nope, q_rope, cache, lengths, w_uk, w_uv):
    scale = (q_nope.shape[2] + q_rope.shape[2]) ** (-0.5) * math.log2(math.e)
    cache_t = jnp.swapaxes(cache, 1, 2)
    vmem = pl.BlockSpec(memory_space=pltpu.VMEM)
    hbm = pl.BlockSpec(memory_space=pl.ANY)
    dma = pltpu.SemaphoreType.DMA
    return pl.pallas_call(
        functools.partial(kernel, scale),
        out_shape=jax.ShapeDtypeStruct((NB, NH * w_uv.shape[2]), BF16),
        in_specs=[hbm] * 6,
        out_specs=vmem,
        scratch_shapes=[
            pltpu.SMEM(lengths.shape, jnp.int32),
            pltpu.VMEM(q_nope.shape, BF16),
            pltpu.VMEM(q_rope.shape, BF16),
            pltpu.VMEM(w_uk.shape, BF16),
            pltpu.VMEM(w_uv.shape, BF16),
            pltpu.VMEM(cache_t.shape, BF16),
            pltpu.VMEM((NB, cache_t.shape[2], 512), BF16),
            pltpu.VMEM((NB, NX, NZ, 16, LANES), BF16),
            pltpu.VMEM((NZ, NX, 8, LANES), BF16),
            pltpu.VMEM((NX * NZ * 16, LANES), F32),
            pltpu.VMEM((NX * NZ * 8, LANES), F32),
            pltpu.VMEM((128, 576), BF16),
            pltpu.VMEM((128, cache_t.shape[2]), F32),
            pltpu.VMEM((128, cache_t.shape[2]), BF16),
            pltpu.VMEM((NB, 128, 512), BF16),
            pltpu.VMEM((NB, NX, 32, 512), BF16),
            pltpu.VMEM((NB, NX, 2, LANES), F32),
            pltpu.VMEM((128, LANES), F32),
            pltpu.VMEM((NB, NZ, 16, LANES), BF16),
            pltpu.VMEM((NB, NZ, 16, LANES), BF16),
            pltpu.VMEM((NB, NZ, 2, LANES), F32),
            pltpu.VMEM((NB * 16, LANES), F32),
            dma((9,)),
            dma((8,)),
            dma((NB + 1,)),
            dma((NB + 1,)),
            dma((NB,)),
            dma((NB,)),
            dma((NB,)),
            dma((NB,)),
        ],
        compiler_params=pltpu.CompilerParams(
            collective_id=0, has_side_effects=True, vmem_limit_bytes=48 * 2**20
        ),
    )(*[pltpu.with_memory_space_constraint(a, pltpu.HBM) for a in (lengths, q_nope, q_rope, w_uk, w_uv, cache_t)])


def solution(mesh):
    in_specs = (
        P("req", "kv", None),
        P("req", "kv", None),
        P("req", "kv", None),
        P("req"),
        P("kv", None, None),
        P("kv", None, None),
    )
    return jax.shard_map(
        local, mesh=mesh, in_specs=in_specs, out_specs=P("req", "kv"), check_vma=False
    )
```
